1024 devices in a mesh: dp: 128 (over z, y), space: 8 (over x, core).
Axes of the slice: x: 4, y: 8, z: 16, core: 2. Of those that a mesh axis runs over, the one named last changes fastest.
Arguments:
- section_three: bfloat16 [128, 32, 32, 768], P('dp', 'space'), may hold values from -6 to 6
- dw_kernel: float32 [7, 7, 768], replicated, may hold values from -0.875 to 0.875
- dw_bias: float32 [768], replicated, may hold values from -3 to 3
- mix_gain: float32 [768], replicated, may hold values from 0.1 to 1.9
- w_expand: bfloat16 [768, 1536], replicated, may hold values from -0.21875 to 0.21875
- w_reduce: bfloat16 [1536, 768], replicated, may hold values from -0.15625 to 0.15625
- layer_scale: float32 [768], replicated, may hold values from 0.3 to 1.5
- down_gain: float32 [768], replicated, may hold values from 0.1 to 1.9
- w_down: bfloat16 [3072, 1536], P(None, 'space'), may hold values from -0.109375 to 0.109375
- owner_table: int32 [128, 256, 1], P('dp'), may hold values from 0 to 127; in each aligned block of 256 rows (0 to 255, 256 to 511, ..., all dimensions but the last counted through in order) at most 2 rows name the same one
- grad_packed: bfloat16 [128, 256, 1536], P('dp', None, 'space'), may hold values from -6 to 6
Outputs:
- packed_tokens: bfloat16 [128, 256, 1536], P('dp', None, 'space')
- grad_mixed: bfloat16 [128, 32, 32, 768], P('dp', 'space')
The draws below stay inside these ranges and needn't reach their ends.
Inputs may be any that keep to these rules, and one draw needn't show every extreme that they name: `owner_table`: among the 256 tokens of one screenshot no owner is named more than 2 times, a bound that some block reaches.
All inputs are finite; a program needn't handle non-finite values.
Results may differ from the reference program's by a relative error of at most 0.018.
Values may be sent and summed in bfloat16 or wider, within the bound.
A program may use at most 32 MiB of HBM per device.

```python
import math
import jax
import jax.numpy as jnp
import numpy as np
from jax import lax

C3 = 768
C4 = 1536
HID = 1536
KS = 7
H3 = 32
W3 = 32
TILES = 256
CAP = 2
SLOTS = 256
N_DP = 128
N_SPACE = 8


def shard_levels(stream_key, extent, pieces, least, largest):
    def one(axis_at, parts):
        heights = jax.random.uniform(jax.random.fold_in(jax.random.fold_in(stream_key, 6), axis_at), (parts,), jnp.float32, least / len(pieces), largest / len(pieces))
        return jnp.repeat(jnp.exp(heights), extent[axis_at] // parts).reshape((-1,) + (1,) * (len(extent) - axis_at - 1))

    level = one(*pieces[0])
    for cut in pieces[1:]:
        level = level * one(*cut)
    return level


def shared_out(key, own, number, rows, amount, top, bound, lean):
    order = jax.random.permutation(key, amount)
    crowded, usual = portions_of(amount, rows * top, bound, lean, True), portions_of(amount, rows * top, bound, lean, False)
    places = jnp.arange(amount)

    def named(tallies, rotation):
        used = int((tallies > 0).sum())
        fixed = max(1, used // 4)
        moved = fixed + (places - fixed + rotation * (used - fixed)) % max(1, amount - fixed)
        return jnp.zeros((amount,), jnp.int32).at[order[jnp.where(places < fixed, places, moved)]].set(jnp.asarray(tallies, jnp.int32))

    tallies = jnp.where(number % 4 == 0, named(crowded, number // 4), named(usual, number - number // 4 - 1))
    mixed = jax.random.permutation(jax.random.fold_in(own, 3), amount)
    giver, receiver = mixed[0:amount // 2 * 2:2], mixed[1:amount // 2 * 2:2]
    room = jnp.minimum(tallies[giver] - 1, bound - tallies[receiver]) // 2
    room = jnp.where((giver == order[0]) | (receiver == order[0]) | (tallies[receiver] == 0), 0, jnp.maximum(room, 0))
    moved = jax.random.randint(jax.random.fold_in(own, 4), (amount // 2,), 0, 1 << 20) % (room + 1)
    tallies = tallies.at[giver].add(-moved).at[receiver].add(moved)
    labels = jnp.searchsorted(jnp.cumsum(tallies), jnp.arange(rows * top), side="right").astype(jnp.int32)
    table = labels.reshape(top, rows).T
    table = table[jax.random.permutation(jax.random.fold_in(own, 1), rows)]
    rotation = jax.random.randint(jax.random.fold_in(own, 2), (rows, 1), 0, top)
    return jnp.take_along_axis(table, (jnp.arange(top)[None, :] + rotation) % top, axis=1)


def portions_of(amount, total, most, slope, full):
    weights = [(1 << 20) // math.isqrt(grade ** slope) + 1 for grade in range(1, amount + 1)]
    largest = most if full else min(most, max(-(-total // amount), total * weights[0] // sum(weights)))
    least = 1 if total - largest >= amount - 1 else 0
    given, spare = [largest] + [least] * (amount - 1), total - largest - least * (amount - 1)
    while spare > 0:
        candidates = [i for i in range(1, amount) if given[i] < largest] or [i for i in range(1, amount) if given[i] < most]
        pool, budget = sum([weights[i] for i in candidates]), spare
        for i in candidates:
            addition = min(most - given[i], max(1, budget * weights[i] // pool), spare)
            given[i] = given[i] + addition
            spare = spare - addition
    return np.array(given)


def bell_draw(key, shape, spread, most, shards=(), kind=jnp.bfloat16):
    drawn = jax.random.normal(key, shape, jnp.float32) * spread
    if len(shards) > 0:
        drawn = shard_levels(key, shape, shards, -0.22, 0.18) * drawn
    return jnp.clip(drawn, min=-most, max=most).astype(kind)


def setup_inputs(seed: int = 0) -> dict:
    keys = jax.random.split(jax.random.key(seed), 12)
    section_three = bell_draw(keys[0], (N_DP, H3, W3, C3), 1.0, 6.0, ((0, 128), (1, 8)))
    dw_kernel = bell_draw(keys[1], (KS, KS, C3), (KS * KS) ** -0.5, 0.875, (), jnp.float32)
    dw_bias = bell_draw(keys[2], (C3,), 0.5, 3.0, (), jnp.float32)
    mix_gain = jnp.clip(1.0 + 0.18 * jax.random.normal(keys[3], (C3,), jnp.float32), 0.1, 1.9)
    w_expand = bell_draw(keys[4], (C3, HID), C3 ** -0.5, 0.21875)
    w_reduce = bell_draw(keys[5], (HID, C3), HID ** -0.5, 0.15625)
    layer_scale = jnp.clip(jnp.exp(jax.random.uniform(keys[6], (C3,), jnp.float32, math.log(0.3), math.log(1.5))), 0.3, 1.5)
    down_gain = jnp.clip(1.0 + 0.18 * jax.random.normal(keys[7], (C3,), jnp.float32), 0.1, 1.9)
    w_down = bell_draw(keys[8], (4 * C3, C4), (4 * C3) ** -0.5, 0.109375, ((1, 8),))
    owner_table_keys = jax.random.split(jax.random.fold_in(keys[9], 1), N_DP * TILES // TILES)
    owner_table_turns = jax.random.permutation(jax.random.fold_in(keys[9], 3), N_DP * TILES // TILES)
    owner_table = jax.vmap(lambda own, number: shared_out(jax.random.fold_in(keys[9], 2), own, number, TILES, N_DP, 1, CAP, 2))(owner_table_keys, owner_table_turns).reshape((N_DP, TILES, 1))
    grad_packed = bell_draw(keys[10], (N_DP, SLOTS, C4), 1.0, 6.0, ((0, 128), (2, 8)))
    return dict(section_three=section_three, dw_kernel=dw_kernel, dw_bias=dw_bias, mix_gain=mix_gain, w_expand=w_expand, w_reduce=w_reduce, layer_scale=layer_scale, down_gain=down_gain, w_down=w_down, owner_table=owner_table, grad_packed=grad_packed)


def depthwise(padded, kernel, height, width):
    total = jnp.zeros((height, width, kernel.shape[2]), jnp.float32)
    for offset_y in range(KS):
        for offset_x in range(KS):
            total = total + padded[offset_y:offset_y + height, offset_x:offset_x + width] * kernel[offset_y, offset_x]
    return total

def layer_norm(values):
    center = values - lax.optimization_barrier(jnp.mean(values, axis=-1, keepdims=True))
    inv_std = lax.rsqrt(lax.optimization_barrier(jnp.mean(center * center, axis=-1, keepdims=True)) + 1e-06)
    return (center * inv_std, inv_std)

def norm_back(grad, normed, inv_std, gain):
    scaled = grad * gain
    return inv_std * (scaled - lax.optimization_barrier(jnp.mean(scaled, axis=-1, keepdims=True)) - normed * lax.optimization_barrier(jnp.mean(scaled * normed, axis=-1, keepdims=True)))

def gelu_slope(pre):
    cumulative = 0.5 * (1.0 + lax.erf(pre * 0.7071067811865476))
    density = jnp.exp(-0.5 * pre * pre) * 0.3989422804014327
    return cumulative + pre * density

def to_patches(grid):
    height, width, channels = grid.shape
    return grid.reshape(height // 2, 2, width // 2, 2, channels).transpose(0, 2, 1, 3, 4).reshape(height // 2 * (width // 2), 4 * channels)

def from_patches(flat, height, width, channels):
    return flat.reshape(height // 2, width // 2, 2, 2, channels).transpose(0, 2, 1, 3, 4).reshape(height, width, channels)

def slot_ranks(targets):
    onehot = (targets[:, None] == jnp.arange(N_DP, dtype=jnp.int32)[None, :]).astype(jnp.int32)
    earlier = (jnp.cumsum(onehot, axis=0) - onehot).astype(jnp.int32)
    return lax.optimization_barrier(jnp.sum(earlier * onehot, axis=1)).astype(jnp.int32)

def reference(section_three, dw_kernel, dw_bias, mix_gain, w_expand, w_reduce, layer_scale, down_gain, w_down, owner_table, grad_packed):
    half = KS // 2

    def forward_parts(shot):
        padded = jnp.pad(shot.astype(jnp.float32), ((half, half), (half, half), (0, 0)))
        mixed = (depthwise(padded, dw_kernel, H3, W3) + dw_bias).reshape(H3 * W3, C3)
        normed_one, inv_one = layer_norm(mixed)
        first = (normed_one * mix_gain).astype(jnp.bfloat16)
        pre = jnp.dot(first, w_expand, preferred_element_type=jnp.float32)
        hidden = jax.nn.gelu(pre, approximate=False).astype(jnp.bfloat16)
        block_out = shot.astype(jnp.float32).reshape(H3 * W3, C3) + layer_scale * jnp.dot(hidden, w_reduce, preferred_element_type=jnp.float32)
        normed_two, inv_two = layer_norm(block_out)
        second = (normed_two * down_gain).astype(jnp.bfloat16)
        return (normed_one, inv_one, pre, normed_two, inv_two, second)

    def forward_shot(shot):
        second = forward_parts(shot)[5]
        patches = to_patches(second.reshape(H3, W3, C3))
        return jnp.dot(patches, w_down, preferred_element_type=jnp.float32).astype(jnp.bfloat16)

    def backward_shot(pair):
        shot, grad_tokens = pair
        normed_one, inv_one, pre, normed_two, inv_two, second = forward_parts(shot)
        group_width = C4 // N_SPACE
        left = grad_tokens.astype(jnp.float32).reshape(TILES, N_SPACE, group_width)
        right = w_down.astype(jnp.float32).reshape(4 * C3, N_SPACE, group_width)
        terms = jnp.einsum('tjc,pjc->jtp', left, right)
        terms = lax.optimization_barrier(terms.astype(jnp.bfloat16))
        grad_patches = lax.optimization_barrier(jnp.sum(terms.astype(jnp.float32), axis=0))
        grad_second = from_patches(grad_patches, H3, W3, C3).reshape(H3 * W3, C3)
        grad_block = norm_back(grad_second, normed_two, inv_two, down_gain)
        grad_scaled = (grad_block * layer_scale).astype(jnp.bfloat16)
        grad_hidden = jnp.dot(grad_scaled, w_reduce.T, preferred_element_type=jnp.float32)
        grad_pre = (grad_hidden * gelu_slope(pre)).astype(jnp.bfloat16)
        grad_first = jnp.dot(grad_pre, w_expand.T, preferred_element_type=jnp.float32)
        grad_mixed = norm_back(grad_first, normed_one, inv_one, mix_gain)
        return grad_mixed.astype(jnp.bfloat16).reshape(H3, W3, C3)
    tokens = lax.map(forward_shot, section_three)
    targets = owner_table[:, :, 0].astype(jnp.int32)
    ranks = jax.vmap(slot_ranks)(targets)
    slots = (jnp.arange(N_DP, dtype=jnp.int32)[:, None] * CAP + ranks).astype(jnp.int32)
    packed_tokens = jnp.zeros((N_DP, SLOTS, C4), jnp.bfloat16).at[targets.reshape(-1), slots.reshape(-1)].set(tokens.reshape(-1, C4))
    grad_tokens = grad_packed[targets, slots]
    grad_mixed = lax.map(backward_shot, (section_three, grad_tokens))
    return (packed_tokens, grad_mixed)
```

```python
import functools

import jax
import jax.numpy as jnp
from jax import lax
from jax.experimental import pallas as pl
from jax.experimental.pallas import tpu as pltpu
from jax.sharding import PartitionSpec as P

KS = 7
HALF = KS // 2
NY = 8
CORES = 2
CAP = 2
EPS = 1e-06
F32 = jnp.float32
BF16 = jnp.bfloat16
MESH = pl.DeviceIdType.MESH


def dot(a, b):
    return jnp.dot(a, b, preferred_element_type=F32)


def dot_nt(a, b):
    return lax.dot_general(a, b, (((1,), (1,)), ((), ())), preferred_element_type=F32)


def dot_tn(a, b):
    return lax.dot_general(a, b, (((0,), (0,)), ((), ())), preferred_element_type=F32)


def log2(n):
    return n.bit_length() - 1


def onehot(picked):
    return jnp.where(picked, 1.0, 0.0).astype(BF16)


def fields(index, *sizes):
    digits = []
    for size in reversed(sizes):
        digits.append(index & (size - 1))
        index = index >> log2(size)
    return digits[::-1]


def norm(v):
    center = v - jnp.mean(v, axis=-1, keepdims=True)
    inv = lax.rsqrt(jnp.mean(center * center, axis=-1, keepdims=True) + EPS)
    return center * inv, inv


def norm_back(grad, normed, inv, gain):
    h = grad * gain
    return inv * (
        h
        - jnp.mean(h, axis=-1, keepdims=True)
        - normed * jnp.mean(h * normed, axis=-1, keepdims=True)
    )


def kernel(
    dims,
    sec_h, dwk_h, bias_h, mixg_h, wexp_h, wred_h, scale_h, downg_h, wdt_h, owner_h, gpt_h,
    tok_o, grad_o,
    ext, dwk, bias, mixg, wexp, wred, scale, downg, wdt, owner, gpt,
    perm, pick, mid_f, mid_b, to_blocks, from_blocks,
    sgz, rgz, sgy, rgy, sty, rty, stz, rtz,
    mixed, normed1, inv1, firstn, firstp, resp, slope, hidden, gpre, proj, normed2, inv2,
    gathered, gtok, pair_s, pair_r, own_f, rs_s, rs_r, gsec, gscaled,
    load_sem, halo_ss, halo_rs, gz_ss, gz_rs, gy_ss, gy_rs, ty_ss, ty_rs, tz_ss, tz_rs,
    ag_ss, ag_rs, fw_ss, fw_rs, pair_ss, pair_rs, rs_ss, rs_rs,
):
    nz, nx, band, width, chans, hid, group, slots = dims
    n_space = nx * CORES
    rows = band * width
    tb = rows // 4
    zrows, yrows = NY * CAP, nz * CAP
    dp, sp = lax.axis_index("dp"), lax.axis_index("space")
    z, y = dp // NY, dp % NY
    x, core = sp // CORES, sp % CORES
    partner = x * CORES + (1 - core)

    def zdev(k):
        return ((z + k) % nz * NY + y, sp)

    def ydev(k):
        return (z * NY + (y + k) % NY, sp)

    def sdev(k):
        return (dp, (sp + k) % n_space)

    def xdev(k):
        return (dp, (x + k) % nx * CORES + core)

    pairs = [
        (sec_h, ext.at[HALF:HALF + band]), (gpt_h, gpt), (owner_h, owner), (dwk_h, dwk),
        (bias_h, bias), (mixg_h, mixg), (wexp_h, wexp), (wred_h, wred),
        (scale_h, scale), (downg_h, downg), (wdt_h, wdt),
    ]
    loads = [pltpu.make_async_copy(a, b, load_sem.at[i]) for i, (a, b) in enumerate(pairs)]
    for load in loads:
        load.start()

    barrier = pltpu.get_barrier_semaphore()

    def greet(count, device):
        @pl.loop(1, count)
        def _(k):
            pl.semaphore_signal(barrier, inc=1, device_id=device(k), device_id_type=MESH)

    greet(nz, zdev)
    greet(NY, ydev)
    greet(n_space, sdev)

    ii = lax.broadcasted_iota(jnp.int32, (slots, slots), 0)
    jj = lax.broadcasted_iota(jnp.int32, (slots, slots), 1)
    q_z, q_y, q_r = fields(ii, nz, NY, CAP)
    mid_f[...] = onehot(jj == q_y * yrows + q_z * CAP + q_r)
    p_y, p_z, p_r = fields(ii, NY, nz, CAP)
    mid_b[...] = onehot(jj == p_z * zrows + p_y * CAP + p_r)
    i2 = lax.broadcasted_iota(jnp.int32, (rows, rows), 0)
    j2 = lax.broadcasted_iota(jnp.int32, (rows, rows), 1)
    a, b, big_r, big_c = fields(i2, 2, 2, band // 2, width // 2)
    to_blocks[...] = onehot(j2 == (2 * big_r + a) * width + 2 * big_c + b)
    big_r, a, big_c, b = fields(i2, band // 2, 2, width // 2, 2)
    from_blocks[...] = onehot(j2 == ((a * 2 + b) * (band // 2) + big_r) * (width // 2) + big_c)

    loads[1].wait()
    sgz[...] = dot_nt(onehot(ii == jj), gpt[...]).astype(BF16)

    loads[2].wait()
    named = jnp.broadcast_to(owner[...].astype(F32), (slots, slots))
    named_col = jnp.sum(jnp.where(ii == jj, named, 0.0), axis=1, keepdims=True)
    rank = jnp.sum(
        jnp.where((named_col == named) & (ii < jj), 1.0, 0.0), axis=0, keepdims=True
    )
    o_z, o_y = fields(owner[...], nz, NY)
    pos = (o_y * yrows + o_z * CAP).astype(F32) + rank
    pos = jnp.broadcast_to(pos, (slots, slots))
    perm[...] = onehot(ii.astype(F32) == pos)
    u_core, u_x, u_i = fields(ii, CORES, nx, tb)
    pos_col = jnp.sum(
        jnp.where(jj == (u_x * CORES + u_core) * tb + u_i, pos, 0.0), axis=1, keepdims=True
    )
    pick[...] = onehot(jj.astype(F32) == pos_col)

    loads[0].wait()

    @pl.when(sp == 0)
    def _():
        ext[0:HALF] = jnp.zeros((HALF, width, chans), BF16)

    @pl.when(sp == n_space - 1)
    def _():
        ext[HALF + band:] = jnp.zeros((HALF, width, chans), BF16)

    pl.semaphore_wait(barrier, nz + NY + n_space - 3)

    def remote(src, dst, ss, rs, device):
        return pltpu.make_async_remote_copy(
            src_ref=src, dst_ref=dst, send_sem=ss, recv_sem=rs,
            device_id=device, device_id_type=MESH,
        )

    up = remote(
        ext.at[HALF:2 * HALF], ext.at[HALF + band:], halo_ss.at[0], halo_rs.at[0],
        (dp, jnp.maximum(sp - 1, 0)),
    )
    down = remote(
        ext.at[band:HALF + band], ext.at[0:HALF], halo_ss.at[1], halo_rs.at[1],
        (dp, jnp.minimum(sp + 1, n_space - 1)),
    )

    @pl.when(sp > 0)
    def _():
        up.start()

    @pl.when(sp < n_space - 1)
    def _():
        down.start()

    def block(k_index, size):
        return pl.ds(pl.multiple_of(k_index * size, size), size)

    def exchange(src, dst, ss, rs, count, me, size, device):
        def copy(k):
            return remote(
                src.at[block((me + k) % count, size)], dst.at[block(me, size)],
                ss.at[k], rs.at[k], device(k),
            )

        def begin():
            @pl.loop(1, count)
            def _(k):
                copy(k).start()

            dst[block(me, size)] = src[block(me, size)]

        def arrive():
            @pl.loop(1, count)
            def _(k):
                copy(k).wait_recv()

        def leave():
            @pl.loop(1, count)
            def _(k):
                copy(k).wait_send()

        return begin, arrive, leave

    gz = exchange(sgz, rgz, gz_ss, gz_rs, nz, z, zrows, zdev)
    gy = exchange(sgy, rgy, gy_ss, gy_rs, NY, y, yrows, ydev)
    ty = exchange(sty, rty, ty_ss, ty_rs, NY, y, yrows, ydev)
    tz = exchange(stz, rtz, tz_ss, tz_rs, nz, z, zrows, zdev)
    gz[0]()

    @pl.when(sp < n_space - 1)
    def _():
        up.wait_recv()

    @pl.when(sp > 0)
    def _():
        down.wait_recv()

    loads[3].wait()
    loads[4].wait()
    loads[5].wait()
    at = lax.broadcasted_iota(jnp.int32, (width, 128), 0)

    @pl.loop(0, chans // 128)
    def _(j):
        lanes = block(j, 128)

        @pl.loop(0, band)
        def _(r):
            acc = [None] * KS
            for dy in range(KS):
                line = ext[r + dy, :, lanes].astype(F32)
                for dx in range(KS):
                    term = line * dwk[dy, dx:dx + 1, lanes]
                    acc[dx] = term if dy == 0 else acc[dx] + term
            total = acc[HALF] + bias[:, lanes]
            for dx in range(KS):
                shift = dx - HALF
                if shift:
                    moved = pltpu.roll(acc[dx], -shift % width, 0)
                    inside = (at + shift >= 0) & (at + shift < width)
                    total = total + jnp.where(inside, moved, 0.0)
            mixed[block(r, width), lanes] = total

    @pl.loop(0, band)
    def _(r):
        at_rows = block(r, width)
        normed, inv = norm(mixed[at_rows, :])
        normed1[at_rows, :] = normed
        inv1[at_rows, :] = inv
        firstn[at_rows, :] = (normed * mixg[...]).astype(BF16)

    firstp[...] = dot(to_blocks[...], firstn[...]).astype(BF16)
    resp[...] = dot(to_blocks[...], ext[HALF:HALF + band].reshape(rows, chans))

    gz[1]()
    sgy[...] = dot(mid_b[...], rgz[...]).astype(BF16)
    gy[0]()

    loads[6].wait()

    @pl.loop(0, hid // 256)
    def _(j):
        cols = block(j, 256)
        pre = dot(firstp[...], wexp[:, cols])
        cumulative = 0.5 * (1.0 + lax.erf(pre * 0.7071067811865476))
        density = jnp.exp(-0.5 * pre * pre) * 0.3989422804014327
        hidden[:, cols] = (pre * cumulative).astype(BF16)
        slope[:, cols] = cumulative + pre * density

    loads[7].wait()

    @pl.loop(0, chans // 256)
    def _(j):
        cols = block(j, 256)
        proj[:, cols] = dot(hidden[...], wred[:, cols])

    loads[8].wait()
    loads[9].wait()
    for q in range(4):
        at_rows = slice(q * tb, (q + 1) * tb)
        normed, inv = norm(resp[at_rows, :] + scale[...] * proj[at_rows, :])
        normed2[at_rows, :] = normed
        inv2[at_rows, :] = inv
        gathered[block(sp, tb), q * chans:(q + 1) * chans] = (normed * downg[...]).astype(BF16)

    def ag(k):
        own = gathered.at[block(sp, tb)]
        return remote(own, own, ag_ss.at[k], ag_rs.at[k], xdev(k))

    def forward(k):
        held = gathered.at[block((x + nx - k) % nx * CORES + core, tb)]
        return remote(held, held, fw_ss.at[k], fw_rs.at[k], (dp, partner))

    for k in range(1, nx):
        ag(k).start()
    forward(0).start()

    gy[1]()
    gtok[...] = dot(pick[...], rgy[...]).astype(BF16)
    loads[10].wait()
    half = nx * tb

    @pl.loop(0, 4 * chans // 512)
    def _(j):
        cols = block(j, 512)
        pair_s[:, cols] = dot(gtok[block(1 - core, half), :], wdt[:, cols]).astype(BF16)

    pair = remote(pair_s, pair_r, pair_ss, pair_rs, (dp, partner))
    pair.start()

    @pl.loop(0, 4 * chans // 512)
    def _(j):
        cols = block(j, 512)
        own_f[:, cols] = dot(gtok[block(core, half), :], wdt[:, cols])

    for k in range(1, nx):
        ag(k).wait_recv()
        forward(k).start()
    pair.wait_recv()

    def scatter(k):
        return remote(
            rs_s.at[block(k, tb)], rs_r.at[block(k, tb)], rs_ss.at[k], rs_rs.at[k], xdev(k)
        )

    for k in range(1, nx):
        there = block((x + k) % nx, tb)
        rs_s[k * tb:(k + 1) * tb, :] = (own_f[there, :] + pair_r[there, :].astype(F32)).astype(BF16)
        scatter(k).start()

    for k in range(nx):
        forward(k).wait_recv()
    tokens = dot_nt(gathered[:, 0:chans], wdt[:, 0:chans])
    for q in range(1, 4):
        cols = slice(q * chans, (q + 1) * chans)
        tokens = tokens + dot_nt(gathered[:, cols], wdt[:, cols])
    sty[...] = dot(perm[...], tokens.astype(BF16)).astype(BF16)
    ty[0]()

    for k in range(1, nx):
        scatter(k).wait_recv()
    here = block(x, tb)
    for q in range(4):
        cols = slice(q * chans, (q + 1) * chans)
        at_rows = slice(q * tb, (q + 1) * tb)
        grad = own_f[here, cols] + pair_r[here, cols].astype(F32)
        for k in range(1, nx):
            grad = grad + rs_r[k * tb:(k + 1) * tb, cols].astype(F32)
        grad = norm_back(grad, normed2[at_rows, :], inv2[at_rows, :], downg[...])
        gscaled[at_rows, :] = (grad * scale[...]).astype(BF16)

    ty[1]()
    stz[...] = dot(mid_f[...], rty[...]).astype(BF16)
    tz[0]()

    @pl.loop(0, hid // 256)
    def _(j):
        cols = block(j, 256)
        grad = dot_nt(gscaled[...], wred[cols, :]) * slope[:, cols]
        gpre[:, cols] = dot(from_blocks[...], grad.astype(BF16)).astype(BF16)

    @pl.loop(0, chans // 256)
    def _(j):
        cols = block(j, 256)
        gsec[:, cols] = dot_nt(gpre[...], wexp[cols, :])

    @pl.loop(0, band)
    def _(r):
        at_rows = block(r, width)
        grad = norm_back(gsec[at_rows, :], normed1[at_rows, :], inv1[at_rows, :], mixg[...])
        grad_o[at_rows, :] = grad.astype(BF16)

    tz[1]()
    tok_o[...] = dot_tn(rtz[...], onehot(ii == jj)).astype(BF16)

    @pl.when(sp > 0)
    def _():
        up.wait_send()

    @pl.when(sp < n_space - 1)
    def _():
        down.wait_send()

    for k in range(1, nx):
        ag(k).wait_send()
        scatter(k).wait_send()
    for k in range(nx):
        forward(k).wait_send()
    pair.wait_send()
    for phase in (gz, gy, ty, tz):
        phase[2]()


def on_device(
    section_three, dw_kernel, dw_bias, mix_gain, w_expand, w_reduce, layer_scale, down_gain,
    w_down, owner_table, grad_packed,
):
    _, band, width, chans = section_three.shape
    hid = w_expand.shape[1]
    group = w_down.shape[1]
    slots = grad_packed.shape[1]
    n_dp, n_space = lax.axis_size("dp"), lax.axis_size("space")
    nz, nx = n_dp // NY, n_space // CORES
    rows = band * width
    tb = rows // 4
    dims = (nz, nx, band, width, chans, hid, group, slots)
    vmem = pltpu.VMEM
    dma = pltpu.SemaphoreType.DMA
    scratch = [
        vmem((band + 2 * HALF, width, chans), BF16),
        vmem((KS, KS, chans), F32), vmem((1, chans), F32), vmem((1, chans), F32),
        vmem((chans, hid), BF16), vmem((hid, chans), BF16), vmem((1, chans), F32),
        vmem((1, chans), F32), vmem((group, 4 * chans), BF16), vmem((1, slots), jnp.int32),
        vmem((group, slots), BF16),
        *[vmem((slots, slots), BF16)] * 4, *[vmem((rows, rows), BF16)] * 2,
        *[vmem((slots, group), BF16)] * 8,
        vmem((rows, chans), F32), vmem((rows, chans), F32), vmem((rows, 1), F32),
        vmem((rows, chans), BF16), vmem((rows, chans), BF16), vmem((rows, chans), F32),
        vmem((rows, hid), F32), vmem((rows, hid), BF16), vmem((rows, hid), BF16),
        vmem((rows, chans), F32), vmem((rows, chans), F32), vmem((rows, 1), F32),
        vmem((n_space * tb, 4 * chans), BF16), vmem((slots, group), BF16),
        vmem((nx * tb, 4 * chans), BF16), vmem((nx * tb, 4 * chans), BF16),
        vmem((nx * tb, 4 * chans), F32),
        vmem((nx * tb, 4 * chans), BF16), vmem((nx * tb, 4 * chans), BF16),
        vmem((rows, chans), F32), vmem((rows, chans), BF16),
        dma((11,)), dma((2,)), dma((2,)),
        dma((nz,)), dma((nz,)), dma((NY,)), dma((NY,)),
        dma((NY,)), dma((NY,)), dma((nz,)), dma((nz,)),
        dma((nx,)), dma((nx,)), dma((nx,)), dma((nx,)), dma, dma, dma((nx,)), dma((nx,)),
    ]
    anywhere = pl.BlockSpec(memory_space=pl.ANY)
    inside = pl.BlockSpec(memory_space=pltpu.VMEM)
    macs = rows * chans * hid * 4 + 2 * slots * group * 4 * chans
    tok, grad = pl.pallas_call(
        functools.partial(kernel, dims),
        out_shape=(
            jax.ShapeDtypeStruct((group, slots), BF16),
            jax.ShapeDtypeStruct((rows, chans), BF16),
        ),
        in_specs=[anywhere] * 11,
        out_specs=(inside, inside),
        scratch_shapes=scratch,
        compiler_params=pltpu.CompilerParams(
            collective_id=0, has_side_effects=True, vmem_limit_bytes=56 * 2**20
        ),
        cost_estimate=pl.CostEstimate(
            flops=2 * macs, bytes_accessed=8 * 2**20, transcendentals=2 * rows * hid
        ),
    )(
        section_three[0], dw_kernel, dw_bias[None], mix_gain[None], w_expand, w_reduce,
        layer_scale[None], down_gain[None], w_down.T, owner_table[:, :, 0], grad_packed[0].T,
    )
    return tok.T[None], grad.reshape(1, band, width, chans)


def solution(mesh):
    in_specs = (
        P("dp", "space", None, None), P(), P(), P(), P(), P(), P(), P(), P(None, "space"),
        P("dp", None, None), P("dp", None, "space"),
    )
    out_specs = (P("dp", None, "space"), P("dp", "space", None, None))
    return jax.shard_map(
        on_device, mesh=mesh, in_specs=in_specs, out_specs=out_specs, check_vma=False
    )
```

```python
import functools

import jax
import jax.numpy as jnp
from jax import lax
from jax.experimental import pallas as pl
from jax.experimental.pallas import tpu as pltpu
from jax.sharding import PartitionSpec as P

KS = 7
HALF = KS // 2
NY = 8
CORES = 2
CAP = 2
EPS = 1e-06
F32 = jnp.float32
BF16 = jnp.bfloat16
MESH = pl.DeviceIdType.MESH


def dot(a, b):
    return jnp.dot(a, b, preferred_element_type=F32)


def dot_nt(a, b):
    return lax.dot_general(a, b, (((1,), (1,)), ((), ())), preferred_element_type=F32)


def dot_tn(a, b):
    return lax.dot_general(a, b, (((0,), (0,)), ((), ())), preferred_element_type=F32)


def log2(n):
    return n.bit_length() - 1


def onehot(picked):
    return jnp.where(picked, 1.0, 0.0).astype(BF16)


def fields(index, *sizes):
    digits = []
    for size in reversed(sizes):
        digits.append(index & (size - 1))
        index = index >> log2(size)
    return digits[::-1]


def norm(v):
    center = v - jnp.mean(v, axis=-1, keepdims=True)
    inv = lax.rsqrt(jnp.mean(center * center, axis=-1, keepdims=True) + EPS)
    return center * inv, inv


def norm_back(grad, normed, inv, gain):
    h = grad * gain
    return inv * (
        h
        - jnp.mean(h, axis=-1, keepdims=True)
        - normed * jnp.mean(h * normed, axis=-1, keepdims=True)
    )


def kernel(
    dims,
    sec_h, dwk_h, bias_h, mixg_h, wexp_h, wred_h, scale_h, downg_h, wdt_h, owner_h, gpt_h,
    tok_o, grad_o,
    ext, dwk, bias, mixg, wexp, wred, scale, downg, wdt, owner, gpt,
    perm, pick, mid_b,
    sgz, rgz, sgy, rgy, st, rt,
    mixed, normed1, inv1, first, slope, hidden, gpre, proj, normed2, inv2, second,
    gathered, gtok, pair_s, pair_r, own_f, rs_s, rs_r, gfirst, gscaled,
    load_sem, halo_ss, halo_rs, gz_ss, gz_rs, gy_ss, gy_rs, t_ss, t_rs,
    ag_ss, ag_rs, fw_ss, fw_rs, pair_ss, pair_rs, rs_ss, rs_rs,
):
    nz, nx, band, width, chans, hid, group, slots = dims
    n_space = nx * CORES
    rows = band * width
    tb = rows // 4
    zrows, yrows = NY * CAP, nz * CAP
    dp, sp = lax.axis_index("dp"), lax.axis_index("space")
    z, y = dp // NY, dp % NY
    x, core = sp // CORES, sp % CORES
    partner = x * CORES + (1 - core)

    def zdev(k):
        return ((z + k) % nz * NY + y, sp)

    def ydev(k):
        return (z * NY + (y + k) % NY, sp)

    def sdev(k):
        return (dp, (sp + k) % n_space)

    def xdev(k):
        return (dp, (x + k) % nx * CORES + core)

    barrier = pltpu.get_barrier_semaphore()

    def greet(count, device):
        @pl.loop(1, count)
        def _(k):
            pl.semaphore_signal(barrier, inc=1, device_id=device(k), device_id_type=MESH)

    greet(n_space, sdev)
    greet(nz, zdev)
    greet(NY, ydev)

    pairs = [
        (sec_h, ext.at[HALF:HALF + band]), (gpt_h, gpt), (owner_h, owner), (dwk_h, dwk),
        (bias_h, bias.at[0]), (mixg_h, mixg.at[0]), (wexp_h, wexp), (wred_h, wred),
        (scale_h, scale.at[0]), (downg_h, downg.at[0]), (wdt_h, wdt),
    ]
    loads = [pltpu.make_async_copy(a, b, load_sem.at[i]) for i, (a, b) in enumerate(pairs)]
    for load in loads:
        load.start()

    ii = lax.broadcasted_iota(jnp.int32, (slots, slots), 0)
    jj = lax.broadcasted_iota(jnp.int32, (slots, slots), 1)
    p_y, p_z, p_r = fields(ii, NY, nz, CAP)
    mid_b[...] = onehot(jj == p_z * zrows + p_y * CAP + p_r)
    loads[1].wait()
    sgz[...] = dot_nt(onehot(ii == jj), gpt[...]).astype(BF16)

    loads[2].wait()
    named = jnp.broadcast_to(owner[...].astype(F32), (slots, slots))
    named_col = jnp.sum(jnp.where(ii == jj, named, 0.0), axis=1, keepdims=True)
    rank = jnp.sum(
        jnp.where((named_col == named) & (ii < jj), 1.0, 0.0), axis=0, keepdims=True
    )
    slot = jnp.broadcast_to((owner[...] * CAP).astype(F32) + rank, (slots, slots))
    perm[...] = onehot(ii.astype(F32) == slot)
    o_z, o_y = fields(owner[...], nz, NY)
    pos = (o_y * yrows + o_z * CAP).astype(F32) + rank
    pos = jnp.broadcast_to(pos, (slots, slots))
    u_core, u_x, u_i = fields(ii, CORES, nx, tb)
    pos_col = jnp.sum(
        jnp.where(jj == (u_x * CORES + u_core) * tb + u_i, pos, 0.0), axis=1, keepdims=True
    )
    pick[...] = onehot(jj.astype(F32) == pos_col)

    loads[0].wait()

    @pl.when(sp == 0)
    def _():
        ext[0:HALF] = jnp.zeros((HALF, width, chans), BF16)

    @pl.when(sp == n_space - 1)
    def _():
        ext[HALF + band:] = jnp.zeros((HALF, width, chans), BF16)

    pl.semaphore_wait(barrier, nz + NY + n_space - 3)

    def remote(src, dst, ss, rs, device):
        return pltpu.make_async_remote_copy(
            src_ref=src, dst_ref=dst, send_sem=ss, recv_sem=rs,
            device_id=device, device_id_type=MESH,
        )

    up = remote(
        ext.at[HALF:2 * HALF], ext.at[HALF + band:], halo_ss.at[0], halo_rs.at[0],
        (dp, jnp.maximum(sp - 1, 0)),
    )
    down = remote(
        ext.at[band:HALF + band], ext.at[0:HALF], halo_ss.at[1], halo_rs.at[1],
        (dp, jnp.minimum(sp + 1, n_space - 1)),
    )

    @pl.when(sp > 0)
    def _():
        up.start()

    @pl.when(sp < n_space - 1)
    def _():
        down.start()

    def block(k_index, size):
        return pl.ds(pl.multiple_of(k_index * size, size), size)

    def exchange(src, dst, ss, rs, count, me, size, device):
        def copy(k):
            return remote(
                src.at[block((me + k) % count, size)], dst.at[block(me, size)],
                ss.at[k], rs.at[k], device(k),
            )

        def begin():
            @pl.loop(1, count)
            def _(k):
                copy(k).start()

            dst[block(me, size)] = src[block(me, size)]

        def arrive():
            @pl.loop(1, count)
            def _(k):
                copy(k).wait_recv()

        def leave():
            @pl.loop(1, count)
            def _(k):
                copy(k).wait_send()

        return begin, arrive, leave

    gz = exchange(sgz, rgz, gz_ss, gz_rs, nz, z, zrows, zdev)
    gy = exchange(sgy, rgy, gy_ss, gy_rs, NY, y, yrows, ydev)
    gz[0]()

    for i in (3, 4, 5):
        loads[i].wait()
    at = lax.broadcasted_iota(jnp.int32, (width, 128), 0)

    def convolve(r, lanes, count, source):
        acc = [None] * KS
        for i in range(count):
            e = source(r, i)
            line = ext[e, :, lanes].astype(F32)
            taps = dwk[e - r, :, lanes]
            for dx in range(KS):
                term = line * taps[dx:dx + 1]
                acc[dx] = term if i == 0 else acc[dx] + term
        total = acc[HALF]
        for dx in range(KS):
            shift = dx - HALF
            if shift:
                moved = pltpu.roll(acc[dx], -shift % width, 0)
                inside = (at + shift >= 0) & (at + shift < width)
                total = total + jnp.where(inside, moved, 0.0)
        return total

    @pl.loop(0, chans // 128)
    def _(j):
        lanes = block(j, 128)

        @pl.loop(0, band)
        def _(r):
            own = convolve(r, lanes, band, lambda r, i: HALF + i)
            mixed[block(r, width), lanes] = own + bias[:, lanes]

    @pl.when(sp < n_space - 1)
    def _():
        up.wait_recv()

    @pl.when(sp > 0)
    def _():
        down.wait_recv()

    @pl.loop(0, chans // 128)
    def _(j):
        lanes = block(j, 128)

        @pl.loop(0, band)
        def _(r):
            at_rows = block(r, width)
            mixed[at_rows, lanes] += convolve(
                r, lanes, HALF, lambda r, i: r + i + band * ((r + i) // HALF)
            )

    @pl.loop(0, band)
    def _(r):
        at_rows = block(r, width)
        normed, inv = norm(mixed[at_rows, :])
        normed1[at_rows, :] = normed
        inv1[at_rows, :] = inv
        first[at_rows, :] = (normed * mixg[...]).astype(BF16)

    loads[6].wait()

    @pl.loop(0, hid // 256)
    def _(j):
        cols = block(j, 256)
        pre = dot(first[...], wexp[:, cols])
        cumulative = 0.5 * (1.0 + lax.erf(pre * 0.7071067811865476))
        density = jnp.exp(-0.5 * pre * pre) * 0.3989422804014327
        hidden[:, cols] = (pre * cumulative).astype(BF16)
        slope[:, cols] = cumulative + pre * density

    loads[7].wait()

    @pl.loop(0, chans // 256)
    def _(j):
        cols = block(j, 256)
        proj[:, cols] = dot(hidden[...], wred[:, cols])

    loads[8].wait()
    loads[9].wait()

    @pl.loop(0, band)
    def _(r):
        at_rows = block(r, width)
        residual = ext[HALF + r].astype(F32)
        normed, inv = norm(residual + scale[...] * proj[at_rows, :])
        inv2[at_rows, :] = jnp.broadcast_to(inv, (width, 128))
        for c in range(chans // 128):
            lanes = slice(c * 128, (c + 1) * 128)
            normed2[c, at_rows, :] = normed[:, lanes]
            second[c, at_rows, :] = normed[:, lanes] * downg[:, lanes]

    def spots(a, b, big_r):
        return pl.ds((2 * big_r + a) * width + b, width // 2, stride=2)

    for a in range(2):
        for b in range(2):
            for c in range(chans // 128):
                lanes = slice((2 * a + b) * chans + c * 128, (2 * a + b) * chans + (c + 1) * 128)
                lines = [second[c, spots(a, b, big_r), :] for big_r in range(band // 2)]
                gathered[block(sp, tb), lanes] = jnp.concatenate(lines, axis=0).astype(BF16)

    right, left, over = (x + 1) % nx, (x + nx - 1) % nx, (x + 2) % nx

    def held(chip, h):
        return gathered.at[pl.ds(pl.multiple_of((chip * CORES + core) * tb + h * (tb // 2), tb // 2), tb // 2)]

    def ag(i, chip, h, target):
        return remote(
            held(chip, h), held(chip, h), ag_ss.at[i], ag_rs.at[i], (dp, target * CORES + core)
        )

    def fw(i, chip, h):
        return remote(held(chip, h), held(chip, h), fw_ss.at[i], fw_rs.at[i], (dp, partner))

    sends = [
        ag(0, x, 0, right), ag(1, x, 1, left), ag(2, x, 1, right), ag(3, x, 0, left),
        ag(4, left, 0, right), ag(5, right, 1, left),
    ]
    passed = [
        fw(0, left, 0), fw(1, right, 1), fw(2, left, 1), fw(3, right, 0),
        fw(4, over, 0), fw(5, over, 1), fw(6, x, 0), fw(7, x, 1),
    ]
    for i in range(4):
        sends[i].start()
    passed[6].start()
    passed[7].start()

    gz[1]()
    sgy[...] = dot(mid_b[...], rgz[...]).astype(BF16)
    gy[0]()

    for i in range(4):
        sends[i].wait_recv()
        if i < 2:
            sends[4 + i].start()
        passed[i].start()

    gy[1]()
    gtok[...] = dot(pick[...], rgy[...]).astype(BF16)
    loads[10].wait()
    half = nx * tb
    parts = [slice(q * chans, (q + 1) * chans) for q in range(4)]

    def pair(q):
        return remote(pair_s.at[q], pair_r.at[q], pair_ss.at[q], pair_rs.at[q], (dp, partner))

    def scatter(q, k):
        to = pl.ds(k * tb, tb)
        return remote(
            rs_s.at[q, to], rs_r.at[q, to], rs_ss.at[q, k], rs_rs.at[q, k], xdev(k)
        )

    for q in range(4):
        pair_s[q] = dot(gtok[block(1 - core, half), :], wdt[:, parts[q]]).astype(BF16)
        pair(q).start()

    for i in range(4, 6):
        sends[i].wait_recv()
        passed[i].start()

    for q in range(4):
        own_f[q] = dot(gtok[block(core, half), :], wdt[:, parts[q]])
        pair(q).wait_recv()
        for k in (2, 1, 3):
            there = block((x + k) % nx, tb)
            rs_s[q, k * tb:(k + 1) * tb, :] = (
                own_f[q, there, :] + pair_r[q, there, :].astype(F32)
            ).astype(BF16)
            scatter(q, k).start()

    for copy in passed:
        copy.wait_recv()
    tokens = dot_nt(gathered[:, 0:chans], wdt[:, 0:chans])
    for q in range(1, 4):
        cols = slice(q * chans, (q + 1) * chans)
        tokens = tokens + dot_nt(gathered[:, cols], wdt[:, cols])
    st[...] = dot(perm[...], tokens.astype(BF16)).astype(BF16).reshape(slots // CAP, CAP, group)

    def token(far_y, far_z):
        def away(far, count):
            return (count // 2 + (1 - 2 * (far % 2)) * ((far + 1) // 2) + count) % count

        o = (z + away(far_z, nz)) % nz * NY + (y + away(far_y, NY)) % NY
        remote(st.at[o], rt.at[dp], t_ss, t_rs, (o, sp)).start()

    @pl.loop(0, NY - 1)
    def _(far_y):
        @pl.loop(0, nz, unroll=nz)
        def _(far_z):
            token(far_y, far_z)

    @pl.loop(0, nz - 1, unroll=nz - 1)
    def _(far_z):
        token(NY - 1, far_z)

    rt[dp] = st[dp]

    here = block(x, tb)
    gain = downg[...]
    for a in range(2):
        for b in range(2):
            q = 2 * a + b
            grad = own_f[q, here, :] + pair_r[q, here, :].astype(F32)
            for k in (1, 3, 2):
                scatter(q, k).wait_recv()
                grad = grad + rs_r[q, k * tb:(k + 1) * tb, :].astype(F32)
            normed = jnp.concatenate([
                jnp.concatenate(
                    [normed2[c, spots(a, b, big_r), :] for c in range(chans // 128)], axis=1
                ) for big_r in range(band // 2)
            ], axis=0)
            inv = jnp.concatenate(
                [inv2[spots(a, b, big_r), :] for big_r in range(band // 2)], axis=0
            )
            grad = norm_back(grad, normed, inv[:, 0:1], gain) * scale[...]
            for big_r in range(band // 2):
                for c in range(chans // 128):
                    second[c, spots(a, b, big_r), :] = grad[
                        big_r * (width // 2):(big_r + 1) * (width // 2), c * 128:(c + 1) * 128
                    ]
    for c in range(chans // 128):
        gscaled[:, c * 128:(c + 1) * 128] = second[c].astype(BF16)

    @pl.loop(0, hid // 256)
    def _(j):
        cols = block(j, 256)
        gpre[:, cols] = (dot_nt(gscaled[...], wred[cols, :]) * slope[:, cols]).astype(BF16)

    @pl.loop(0, chans // 256)
    def _(j):
        cols = block(j, 256)
        gfirst[:, cols] = dot_nt(gpre[...], wexp[cols, :])

    @pl.loop(0, band)
    def _(r):
        at_rows = block(r, width)
        grad = norm_back(gfirst[at_rows, :], normed1[at_rows, :], inv1[at_rows, :], mixg[...])
        grad_o[at_rows, :] = grad.astype(BF16)

    every = slots // CAP - 1
    came = remote(st.at[0:every], rt.at[0:every], t_ss, t_rs, (dp, partner))
    came.wait_recv()
    tok_o[...] = dot_tn(rt[...].reshape(slots, group), onehot(ii == jj)).astype(BF16)

    @pl.when(sp > 0)
    def _():
        up.wait_send()

    @pl.when(sp < n_space - 1)
    def _():
        down.wait_send()

    for q in range(4):
        pair(q).wait_send()
        for k in range(1, nx):
            scatter(q, k).wait_send()
    for copy in (*sends, *passed):
        copy.wait_send()
    came.wait_send()
    for phase in (gz, gy):
        phase[2]()


def on_device(
    section_three, dw_kernel, dw_bias, mix_gain, w_expand, w_reduce, layer_scale, down_gain,
    w_down, owner_table, grad_packed,
):
    _, band, width, chans = section_three.shape
    hid = w_expand.shape[1]
    group = w_down.shape[1]
    slots = grad_packed.shape[1]
    n_dp, n_space = lax.axis_size("dp"), lax.axis_size("space")
    nz, nx = n_dp // NY, n_space // CORES
    rows = band * width
    tb = rows // 4
    dims = (nz, nx, band, width, chans, hid, group, slots)
    vmem = pltpu.VMEM
    dma = pltpu.SemaphoreType.DMA
    scratch = [
        vmem((band + 2 * HALF, width, chans), BF16),
        vmem((KS, KS, chans), F32), vmem((1, chans), F32), vmem((1, chans), F32),
        vmem((chans, hid), BF16), vmem((hid, chans), BF16), vmem((1, chans), F32),
        vmem((1, chans), F32), vmem((group, 4 * chans), BF16), vmem((1, slots), jnp.int32),
        vmem((group, slots), BF16),
        *[vmem((slots, slots), BF16)] * 3,
        *[vmem((slots, group), BF16)] * 4, *[vmem((slots // CAP, CAP, group), BF16)] * 2,
        vmem((rows, chans), F32), vmem((rows, chans), F32), vmem((rows, 1), F32),
        vmem((rows, chans), BF16), vmem((rows, hid), F32), vmem((rows, hid), BF16),
        vmem((rows, hid), BF16), vmem((rows, chans), F32),
        vmem((chans // 128, rows, 128), F32), vmem((rows, 128), F32),
        vmem((chans // 128, rows, 128), F32),
        vmem((n_space * tb, 4 * chans), BF16), vmem((slots, group), BF16),
        vmem((4, nx * tb, chans), BF16), vmem((4, nx * tb, chans), BF16),
        vmem((4, nx * tb, chans), F32),
        vmem((4, nx * tb, chans), BF16), vmem((4, nx * tb, chans), BF16),
        vmem((rows, chans), F32), vmem((rows, chans), BF16),
        dma((11,)), dma((2,)), dma((2,)),
        dma((nz,)), dma((nz,)), dma((NY,)), dma((NY,)),
        dma, dma, dma((6,)), dma((6,)), dma((8,)), dma((8,)), dma((4,)), dma((4,)),
        dma((4, nx)), dma((4, nx)),
    ]
    anywhere = pl.BlockSpec(memory_space=pl.ANY)
    inside = pl.BlockSpec(memory_space=pltpu.VMEM)
    macs = rows * chans * hid * 4 + 2 * slots * group * 4 * chans
    tok, grad = pl.pallas_call(
        functools.partial(kernel, dims),
        out_shape=(vmem((group, slots), BF16), vmem((rows, chans), BF16)),
        in_specs=[anywhere] * 11,
        out_specs=(inside, inside),
        scratch_shapes=scratch,
        compiler_params=pltpu.CompilerParams(
            collective_id=0, has_side_effects=True, vmem_limit_bytes=56 * 2**20
        ),
        cost_estimate=pl.CostEstimate(
            flops=2 * macs, bytes_accessed=8 * 2**20, transcendentals=2 * rows * hid
        ),
    )(
        section_three[0], dw_kernel, dw_bias, mix_gain, w_expand, w_reduce,
        layer_scale, down_gain, w_down.T, owner_table[:, :, 0], grad_packed[0].T,
    )
    return tok.T[None], grad.reshape(1, band, width, chans)


def solution(mesh):
    in_specs = (
        P("dp", "space", None, None), P(), P(), P(), P(), P(), P(), P(), P(None, "space"),
        P("dp", None, None), P("dp", None, "space"),
    )
    out_specs = (P("dp", None, "space"), P("dp", "space", None, None))
    return jax.shard_map(
        on_device, mesh=mesh, in_specs=in_specs, out_specs=out_specs, check_vma=False
    )
```

```python
import functools

import jax
import jax.numpy as jnp
from jax import lax
from jax.experimental import pallas as pl
from jax.experimental.pallas import tpu as pltpu
from jax.sharding import PartitionSpec as P

KS = 7
HALF = KS // 2
NY = 8
CORES = 2
CAP = 2
EPS = 1e-06
F32 = jnp.float32
BF16 = jnp.bfloat16
MESH = pl.DeviceIdType.MESH


def dot(a, b):
    return jnp.dot(a, b, preferred_element_type=F32)


def dot_nt(a, b):
    return lax.dot_general(a, b, (((1,), (1,)), ((), ())), preferred_element_type=F32)


def dot_tn(a, b):
    return lax.dot_general(a, b, (((0,), (0,)), ((), ())), preferred_element_type=F32)


def log2(n):
    return n.bit_length() - 1


def onehot(picked):
    return jnp.where(picked, 1.0, 0.0).astype(BF16)


def fields(index, *sizes):
    digits = []
    for size in reversed(sizes):
        digits.append(index & (size - 1))
        index = index >> log2(size)
    return digits[::-1]


def norm(v):
    center = v - jnp.mean(v, axis=-1, keepdims=True)
    inv = lax.rsqrt(jnp.mean(center * center, axis=-1, keepdims=True) + EPS)
    return center * inv, inv


def norm_back(grad, normed, inv, gain):
    h = grad * gain
    return inv * (
        h
        - jnp.mean(h, axis=-1, keepdims=True)
        - normed * jnp.mean(h * normed, axis=-1, keepdims=True)
    )


def kernel(
    dims,
    sec_h, dwk_h, bias_h, mixg_h, wexp_h, wred_h, scale_h, downg_h, wdt_h, owner_h, gpt_h,
    tok_o, grad_o,
    ext, dwk, bias, mixg, wexp, wred, scale, downg, wdt, owner, gpt,
    perm, pick, middle,
    sgy, rgy, sgz, rgz, st, rt,
    mixed, normed1, inv1, first, slope, hidden, gpre, proj, normed2, inv2, second,
    gathered, gtok, pair_s, pair_r, own_f, rs_s, rs_r, gfirst, gscaled,
    load_sem, halo_ss, halo_rs, gy_ss, gy_rs, gz_ss, gz_rs, t_ss, t_rs,
    ag_ss, ag_rs, fw_ss, fw_rs, pair_ss, pair_rs, rs_ss, rs_rs, known,
):
    nz, nx, band, width, chans, hid, group, slots = dims
    n_space = nx * CORES
    rows = band * width
    tb = rows // 4
    zrows, yrows = NY * CAP, nz * CAP
    dp, sp = lax.axis_index("dp"), lax.axis_index("space")
    z, y = dp // NY, dp % NY
    x, core = sp // CORES, sp % CORES
    partner = x * CORES + (1 - core)

    def zdev(k):
        return ((z + k) % nz * NY + y, sp)

    def ydev(k):
        return (z * NY + (y + k) % NY, sp)

    def sdev(k):
        return (dp, (sp + k) % n_space)

    def xdev(k):
        return (dp, (x + k) % nx * CORES + core)

    barrier = pltpu.get_barrier_semaphore()

    near_z = sorted({k % nz for k in (1, -1, 3, -3, 4, -4)} - {0})
    for device, away in ((sdev, range(1, n_space)), (ydev, range(1, NY)), (zdev, near_z)):
        for k in away:
            pl.semaphore_signal(barrier, inc=1, device_id=device(k), device_id_type=MESH)

    pairs = [
        (sec_h, ext.at[HALF:HALF + band]), (gpt_h, gpt), (owner_h, owner), (dwk_h, dwk),
        (bias_h, bias.at[0]), (mixg_h, mixg.at[0]), (wexp_h, wexp), (wred_h, wred),
        (scale_h, scale.at[0]), (downg_h, downg.at[0]), (wdt_h, wdt),
    ]
    loads = [pltpu.make_async_copy(a, b, load_sem.at[i]) for i, (a, b) in enumerate(pairs)]
    for load in loads:
        load.start()

    ii = lax.broadcasted_iota(jnp.int32, (slots, slots), 0)
    jj = lax.broadcasted_iota(jnp.int32, (slots, slots), 1)
    q_z, q_y, q_r = fields(ii, nz, NY, CAP)
    middle[...] = onehot(jj == q_y * yrows + q_z * CAP + q_r)
    p_y, p_z, p_r = fields(ii, NY, nz, CAP)
    by_y = onehot(jj == p_z * zrows + p_y * CAP + p_r)

    loads[1].wait()
    sgy[...] = dot_nt(by_y, gpt[...]).astype(BF16)

    loads[2].wait()
    named = jnp.broadcast_to(owner[...].astype(F32), (slots, slots))
    named_col = jnp.sum(jnp.where(ii == jj, named, 0.0), axis=1, keepdims=True)
    rank = jnp.sum(
        jnp.where((named_col == named) & (ii < jj), 1.0, 0.0), axis=0, keepdims=True
    )
    slot = jnp.broadcast_to((owner[...] * CAP).astype(F32) + rank, (slots, slots))
    perm[...] = onehot(ii.astype(F32) == slot)
    u_core, u_x, u_i = fields(ii, CORES, nx, tb)
    pos_col = jnp.sum(
        jnp.where(jj == (u_x * CORES + u_core) * tb + u_i, slot, 0.0), axis=1, keepdims=True
    )
    pick[...] = onehot(jj.astype(F32) == pos_col)

    loads[0].wait()

    @pl.when(sp == 0)
    def _():
        ext[0:HALF] = jnp.zeros((HALF, width, chans), BF16)

    @pl.when(sp == n_space - 1)
    def _():
        ext[HALF + band:] = jnp.zeros((HALF, width, chans), BF16)

    pl.semaphore_wait(barrier, n_space - 1 + NY - 1 + len(near_z))
    for k in near_z:
        pl.semaphore_signal(known, inc=1, device_id=zdev(k), device_id_type=MESH)

    def remote(src, dst, ss, rs, device):
        return pltpu.make_async_remote_copy(
            src_ref=src, dst_ref=dst, send_sem=ss, recv_sem=rs,
            device_id=device, device_id_type=MESH,
        )

    up = remote(
        ext.at[HALF:2 * HALF], ext.at[HALF + band:], halo_ss.at[0], halo_rs.at[0],
        (dp, jnp.maximum(sp - 1, 0)),
    )
    down = remote(
        ext.at[band:HALF + band], ext.at[0:HALF], halo_ss.at[1], halo_rs.at[1],
        (dp, jnp.minimum(sp + 1, n_space - 1)),
    )

    @pl.when(sp > 0)
    def _():
        up.start()

    @pl.when(sp < n_space - 1)
    def _():
        down.start()

    def block(k_index, size):
        return pl.ds(pl.multiple_of(k_index * size, size), size)

    def far_first(count):
        return sorted(range(1, count), key=lambda k: -min(k, count - k))

    def exchange(src, dst, ss, rs, count, me, size, device):
        def begin():
            for k in far_first(count):
                there = block((me + k) % count, size)
                remote(src.at[there], dst.at[block(me, size)], ss, rs, device(k)).start()
            dst[block(me, size)] = src[block(me, size)]

        others = pl.ds(0, (count - 1) * size)
        return begin, remote(src.at[others], dst.at[others], ss, rs, (dp, partner))

    grads_y, came_y = exchange(sgy, rgy, gy_ss, gy_rs, NY, y, yrows, ydev)
    grads_z, came_z = exchange(sgz, rgz, gz_ss, gz_rs, nz, z, zrows, zdev)
    grads_y()

    for i in (3, 4, 5):
        loads[i].wait()
    at = lax.broadcasted_iota(jnp.int32, (width, 128), 0)

    def convolve(r, lanes, count, source):
        acc = [None] * KS
        for i in range(count):
            e = source(r, i)
            line = ext[e, :, lanes].astype(F32)
            taps = dwk[e - r, :, lanes]
            for dx in range(KS):
                term = line * taps[dx:dx + 1]
                acc[dx] = term if i == 0 else acc[dx] + term
        total = acc[HALF]
        for dx in range(KS):
            shift = dx - HALF
            if shift:
                moved = pltpu.roll(acc[dx], -shift % width, 0)
                inside = (at + shift >= 0) & (at + shift < width)
                total = total + jnp.where(inside, moved, 0.0)
        return total

    @pl.loop(0, chans // 128)
    def _(j):
        lanes = block(j, 128)

        @pl.loop(0, band)
        def _(r):
            own = convolve(r, lanes, band, lambda r, i: HALF + i)
            mixed[block(r, width), lanes] = own + bias[:, lanes]

    @pl.when(sp < n_space - 1)
    def _():
        up.wait_recv()

    @pl.when(sp > 0)
    def _():
        down.wait_recv()

    @pl.loop(0, chans // 128)
    def _(j):
        lanes = block(j, 128)

        @pl.loop(0, band)
        def _(r):
            at_rows = block(r, width)
            mixed[at_rows, lanes] += convolve(
                r, lanes, HALF, lambda r, i: r + i + band * ((r + i) // HALF)
            )

    @pl.loop(0, band, unroll=True)
    def _(r):
        at_rows = block(r, width)
        normed, inv = norm(mixed[at_rows, :])
        normed1[at_rows, :] = normed
        inv1[at_rows, :] = inv
        first[at_rows, :] = (normed * mixg[...]).astype(BF16)

    loads[6].wait()

    @pl.loop(0, hid // 256, unroll=True)
    def _(j):
        cols = block(j, 256)
        pre = dot(first[...], wexp[:, cols])
        cumulative = 0.5 * (1.0 + lax.erf(pre * 0.7071067811865476))
        density = jnp.exp(-0.5 * pre * pre) * 0.3989422804014327
        hidden[:, cols] = (pre * cumulative).astype(BF16)
        slope[:, cols] = cumulative + pre * density

    loads[7].wait()

    @pl.loop(0, chans // 256, unroll=True)
    def _(j):
        cols = block(j, 256)
        proj[:, cols] = dot(hidden[...], wred[:, cols])

    loads[8].wait()
    loads[9].wait()

    @pl.loop(0, band, unroll=True)
    def _(r):
        at_rows = block(r, width)
        residual = ext[HALF + r].astype(F32)
        normed, inv = norm(residual + scale[...] * proj[at_rows, :])
        inv2[at_rows, :] = jnp.broadcast_to(inv, (width, 128))
        for c in range(chans // 128):
            lanes = slice(c * 128, (c + 1) * 128)
            normed2[c, at_rows, :] = normed[:, lanes]
            second[c, at_rows, :] = normed[:, lanes] * downg[:, lanes]

    def spots(a, b, big_r):
        return pl.ds((2 * big_r + a) * width + b, width // 2, stride=2)

    for a in range(2):
        for b in range(2):
            for c in range(chans // 128):
                lanes = slice((2 * a + b) * chans + c * 128, (2 * a + b) * chans + (c + 1) * 128)
                lines = [second[c, spots(a, b, big_r), :] for big_r in range(band // 2)]
                gathered[block(sp, tb), lanes] = jnp.concatenate(lines, axis=0).astype(BF16)

    right, left, over = (x + 1) % nx, (x + nx - 1) % nx, (x + 2) % nx

    def held(chip, h):
        return gathered.at[pl.ds(pl.multiple_of((chip * CORES + core) * tb + h * (tb // 2), tb // 2), tb // 2)]

    def ag(i, chip, h, target):
        return remote(
            held(chip, h), held(chip, h), ag_ss.at[i], ag_rs.at[i], (dp, target * CORES + core)
        )

    def fw(i, chip, h):
        return remote(held(chip, h), held(chip, h), fw_ss.at[i], fw_rs.at[i], (dp, partner))

    sends = [
        ag(0, x, 0, right), ag(1, x, 1, left), ag(2, x, 1, right), ag(3, x, 0, left),
        ag(4, left, 0, right), ag(5, right, 1, left),
    ]
    passed = [
        fw(0, left, 0), fw(1, right, 1), fw(2, left, 1), fw(3, right, 0),
        fw(4, over, 0), fw(5, over, 1), fw(6, x, 0), fw(7, x, 1),
    ]
    for i in range(4):
        sends[i].start()
    passed[6].start()
    passed[7].start()

    pl.semaphore_wait(known, len(near_z))
    came_y.wait_recv()
    sgz[...] = dot(middle[...], rgy[...]).astype(BF16)
    grads_z()

    for i in range(4):
        sends[i].wait_recv()
        if i < 2:
            sends[4 + i].start()
        passed[i].start()

    came_z.wait_recv()
    gtok[...] = dot(pick[...], rgz[...]).astype(BF16)
    loads[10].wait()
    half = nx * tb
    parts = [slice(q * chans, (q + 1) * chans) for q in range(4)]

    def pair(q):
        return remote(pair_s.at[q], pair_r.at[q], pair_ss.at[q], pair_rs.at[q], (dp, partner))

    def scatter(q, k):
        to = pl.ds(k * tb, tb)
        return remote(
            rs_s.at[q, to], rs_r.at[q, to], rs_ss.at[q, k], rs_rs.at[q, k], xdev(k)
        )

    for q in range(4):
        pair_s[q] = dot(gtok[block(1 - core, half), :], wdt[:, parts[q]]).astype(BF16)
        pair(q).start()

    for i in range(4, 6):
        sends[i].wait_recv()
        passed[i].start()

    for q in range(4):
        own_f[q] = dot(gtok[block(core, half), :], wdt[:, parts[q]])
        pair(q).wait_recv()
        for k in (2, 1, 3):
            there = block((x + k) % nx, tb)
            rs_s[q, k * tb:(k + 1) * tb, :] = (
                own_f[q, there, :] + pair_r[q, there, :].astype(F32)
            ).astype(BF16)
            scatter(q, k).start()

    for copy in passed:
        copy.wait_recv()
    tokens = dot_nt(gathered[:, 0:chans], wdt[:, 0:chans])
    for q in range(1, 4):
        cols = slice(q * chans, (q + 1) * chans)
        tokens = tokens + dot_nt(gathered[:, cols], wdt[:, cols])
    st[...] = dot(perm[...], tokens.astype(BF16)).astype(BF16).reshape(slots // CAP, CAP, group)

    def token(far_y, far_z):
        def away(far, count):
            return (count // 2 + (1 - 2 * (far % 2)) * ((far + 1) // 2) + count) % count

        o = (z + away(far_z, nz)) % nz * NY + (y + away(far_y, NY)) % NY
        remote(st.at[o], rt.at[dp], t_ss, t_rs, (o, sp)).start()

    @pl.loop(0, NY - 1)
    def _(far_y):
        @pl.loop(0, nz, unroll=nz)
        def _(far_z):
            token(far_y, far_z)

    @pl.loop(0, nz - 1, unroll=nz - 1)
    def _(far_z):
        token(NY - 1, far_z)

    rt[dp] = st[dp]

    here = block(x, tb)
    gain = downg[...]
    for a in range(2):
        for b in range(2):
            q = 2 * a + b
            grad = own_f[q, here, :] + pair_r[q, here, :].astype(F32)
            for k in (1, 3, 2):
                scatter(q, k).wait_recv()
                grad = grad + rs_r[q, k * tb:(k + 1) * tb, :].astype(F32)
            normed = jnp.concatenate([
                jnp.concatenate(
                    [normed2[c, spots(a, b, big_r), :] for c in range(chans // 128)], axis=1
                ) for big_r in range(band // 2)
            ], axis=0)
            inv = jnp.concatenate(
                [inv2[spots(a, b, big_r), :] for big_r in range(band // 2)], axis=0
            )
            grad = norm_back(grad, normed, inv[:, 0:1], gain) * scale[...]
            for big_r in range(band // 2):
                for c in range(chans // 128):
                    second[c, spots(a, b, big_r), :] = grad[
                        big_r * (width // 2):(big_r + 1) * (width // 2), c * 128:(c + 1) * 128
                    ]
    for c in range(chans // 128):
        gscaled[:, c * 128:(c + 1) * 128] = second[c].astype(BF16)

    @pl.loop(0, hid // 256, unroll=True)
    def _(j):
        cols = block(j, 256)
        gpre[:, cols] = (dot_nt(gscaled[...], wred[cols, :]) * slope[:, cols]).astype(BF16)

    @pl.loop(0, chans // 256, unroll=True)
    def _(j):
        cols = block(j, 256)
        gfirst[:, cols] = dot_nt(gpre[...], wexp[cols, :])

    @pl.loop(0, band, unroll=True)
    def _(r):
        at_rows = block(r, width)
        grad = norm_back(gfirst[at_rows, :], normed1[at_rows, :], inv1[at_rows, :], mixg[...])
        grad_o[at_rows, :] = grad.astype(BF16)

    every = slots // CAP - 1
    came = remote(st.at[0:every], rt.at[0:every], t_ss, t_rs, (dp, partner))
    came.wait_recv()
    tok_o[...] = dot_tn(rt[...].reshape(slots, group), onehot(ii == jj)).astype(BF16)

    @pl.when(sp > 0)
    def _():
        up.wait_send()

    @pl.when(sp < n_space - 1)
    def _():
        down.wait_send()

    for q in range(4):
        pair(q).wait_send()
        for k in range(1, nx):
            scatter(q, k).wait_send()
    for copy in (*sends, *passed):
        copy.wait_send()
    came.wait_send()
    came_y.wait_send()
    came_z.wait_send()


def on_device(
    section_three, dw_kernel, dw_bias, mix_gain, w_expand, w_reduce, layer_scale, down_gain,
    w_down, owner_table, grad_packed,
):
    _, band, width, chans = section_three.shape
    hid = w_expand.shape[1]
    group = w_down.shape[1]
    slots = grad_packed.shape[1]
    n_dp, n_space = lax.axis_size("dp"), lax.axis_size("space")
    nz, nx = n_dp // NY, n_space // CORES
    rows = band * width
    tb = rows // 4
    dims = (nz, nx, band, width, chans, hid, group, slots)
    vmem = pltpu.VMEM
    dma = pltpu.SemaphoreType.DMA
    scratch = [
        vmem((band + 2 * HALF, width, chans), BF16),
        vmem((KS, KS, chans), F32), vmem((1, chans), F32), vmem((1, chans), F32),
        vmem((chans, hid), BF16), vmem((hid, chans), BF16), vmem((1, chans), F32),
        vmem((1, chans), F32), vmem((group, 4 * chans), BF16), vmem((1, slots), jnp.int32),
        vmem((group, slots), BF16),
        *[vmem((slots, slots), BF16)] * 3,
        *[vmem((slots, group), BF16)] * 4, *[vmem((slots // CAP, CAP, group), BF16)] * 2,
        vmem((rows, chans), F32), vmem((rows, chans), F32), vmem((rows, 1), F32),
        vmem((rows, chans), BF16), vmem((rows, hid), F32), vmem((rows, hid), BF16),
        vmem((rows, hid), BF16), vmem((rows, chans), F32),
        vmem((chans // 128, rows, 128), F32), vmem((rows, 128), F32),
        vmem((chans // 128, rows, 128), F32),
        vmem((n_space * tb, 4 * chans), BF16), vmem((slots, group), BF16),
        vmem((4, nx * tb, chans), BF16), vmem((4, nx * tb, chans), BF16),
        vmem((4, nx * tb, chans), F32),
        vmem((4, nx * tb, chans), BF16), vmem((4, nx * tb, chans), BF16),
        vmem((rows, chans), F32), vmem((rows, chans), BF16),
        dma((11,)), dma((2,)), dma((2,)),
        dma, dma, dma, dma, dma, dma, dma((6,)), dma((6,)), dma((8,)), dma((8,)), dma((4,)), dma((4,)),
        dma((4, nx)), dma((4, nx)), pltpu.SemaphoreType.REGULAR,
    ]
    anywhere = pl.BlockSpec(memory_space=pl.ANY)
    inside = pl.BlockSpec(memory_space=pltpu.VMEM)
    macs = rows * chans * hid * 4 + 2 * slots * group * 4 * chans
    tok, grad = pl.pallas_call(
        functools.partial(kernel, dims),
        out_shape=(vmem((group, slots), BF16), vmem((rows, chans), BF16)),
        in_specs=[anywhere] * 11,
        out_specs=(inside, inside),
        scratch_shapes=scratch,
        compiler_params=pltpu.CompilerParams(
            collective_id=0, has_side_effects=True, vmem_limit_bytes=56 * 2**20
        ),
        cost_estimate=pl.CostEstimate(
            flops=2 * macs, bytes_accessed=8 * 2**20, transcendentals=2 * rows * hid
        ),
    )(
        section_three[0], dw_kernel, dw_bias, mix_gain, w_expand, w_reduce,
        layer_scale, down_gain, w_down.T, owner_table[:, :, 0], grad_packed[0].T,
    )
    return tok.T[None], grad.reshape(1, band, width, chans)


def solution(mesh):
    in_specs = (
        P("dp", "space", None, None), P(), P(), P(), P(), P(), P(), P(), P(None, "space"),
        P("dp", None, None), P("dp", None, "space"),
    )
    out_specs = (P("dp", None, "space"), P("dp", "space", None, None))
    return jax.shard_map(
        on_device, mesh=mesh, in_specs=in_specs, out_specs=out_specs, check_vma=False
    )
```

```python
import functools

import jax
import jax.numpy as jnp
from jax import lax
from jax.experimental import pallas as pl
from jax.experimental.pallas import tpu as pltpu
from jax.sharding import PartitionSpec as P

KS = 7
HALF = KS // 2
NY = 8
CORES = 2
CAP = 2
EPS = 1e-06
F32 = jnp.float32
BF16 = jnp.bfloat16
MESH = pl.DeviceIdType.MESH


def dot(a, b):
    return jnp.dot(a, b, preferred_element_type=F32)


def dot_nt(a, b):
    return lax.dot_general(a, b, (((1,), (1,)), ((), ())), preferred_element_type=F32)


def dot_tn(a, b):
    return lax.dot_general(a, b, (((0,), (0,)), ((), ())), preferred_element_type=F32)


def log2(n):
    return n.bit_length() - 1


def onehot(picked):
    return jnp.where(picked, 1.0, 0.0).astype(BF16)


def fields(index, *sizes):
    digits = []
    for size in reversed(sizes):
        digits.append(index & (size - 1))
        index = index >> log2(size)
    return digits[::-1]


def norm(v):
    center = v - jnp.mean(v, axis=-1, keepdims=True)
    inv = lax.rsqrt(jnp.mean(center * center, axis=-1, keepdims=True) + EPS)
    return center * inv, inv


def norm_back(grad, normed, inv, gain):
    h = grad * gain
    return inv * (
        h
        - jnp.mean(h, axis=-1, keepdims=True)
        - normed * jnp.mean(h * normed, axis=-1, keepdims=True)
    )


def kernel(
    dims,
    sec_h, dwk_h, bias_h, mixg_h, wexp_h, wred_h, scale_h, downg_h, wdt_h, owner_h, gpt_h,
    tok_o, grad_o,
    ext, dwk, bias, mixg, wexp, wred, scale, downg, wdt, owner, gpt,
    perm, pick, middle,
    sgy, rgy, sgz, rgz, st, rt,
    mixed, normed1, inv1, first, slope, hidden, gpre, proj, normed2, inv2, second,
    gathered, gtok, pair_s, pair_r, own_f, rs_s, rs_r, gfirst, gscaled,
    load_sem, halo_ss, halo_rs, gy_ss, gy_rs, gz_ss, gz_rs, t_ss, t_rs,
    ag_ss, ag_rs, fw_ss, fw_rs, pair_ss, pair_rs, rs_ss, rs_rs, known,
):
    nz, nx, band, width, chans, hid, group, slots = dims
    n_space = nx * CORES
    rows = band * width
    tb = rows // 4
    zrows, yrows = NY * CAP, nz * CAP
    dp, sp = lax.axis_index("dp"), lax.axis_index("space")
    z, y = dp // NY, dp % NY
    x, core = sp // CORES, sp % CORES
    partner = x * CORES + (1 - core)

    def zdev(k):
        return ((z + k) % nz * NY + y, sp)

    def ydev(k):
        return (z * NY + (y + k) % NY, sp)

    def sdev(k):
        return (dp, (sp + k) % n_space)

    def xdev(k):
        return (dp, (x + k) % nx * CORES + core)

    barrier = pltpu.get_barrier_semaphore()

    near_z = sorted({k % nz for k in (1, -1, 3, -3, 4, -4)} - {0})
    for device, away in ((sdev, range(1, n_space)), (ydev, range(1, NY)), (zdev, near_z)):
        for k in away:
            pl.semaphore_signal(barrier, inc=1, device_id=device(k), device_id_type=MESH)

    pairs = [
        (sec_h, ext.at[HALF:HALF + band]), (gpt_h, gpt), (owner_h, owner), (dwk_h, dwk),
        (bias_h, bias.at[0]), (mixg_h, mixg.at[0]), (wexp_h, wexp), (wred_h, wred),
        (scale_h, scale.at[0]), (downg_h, downg.at[0]), (wdt_h, wdt),
    ]
    loads = [pltpu.make_async_copy(a, b, load_sem.at[i]) for i, (a, b) in enumerate(pairs)]
    for load in loads:
        load.start()

    ii = lax.broadcasted_iota(jnp.int32, (slots, slots), 0)
    jj = lax.broadcasted_iota(jnp.int32, (slots, slots), 1)
    p_y, p_z, p_r = fields(ii, NY, nz, CAP)
    by_y = onehot(jj == p_z * zrows + p_y * CAP + p_r)

    loads[1].wait()
    sgy[...] = dot_nt(by_y, gpt[...]).astype(BF16)

    loads[0].wait()

    @pl.when(sp == 0)
    def _():
        ext[0:HALF] = jnp.zeros((HALF, width, chans), BF16)

    @pl.when(sp == n_space - 1)
    def _():
        ext[HALF + band:] = jnp.zeros((HALF, width, chans), BF16)

    pl.semaphore_wait(barrier, n_space - 1 + NY - 1 + len(near_z))
    for k in near_z:
        pl.semaphore_signal(known, inc=1, device_id=zdev(k), device_id_type=MESH)

    def remote(src, dst, ss, rs, device):
        return pltpu.make_async_remote_copy(
            src_ref=src, dst_ref=dst, send_sem=ss, recv_sem=rs,
            device_id=device, device_id_type=MESH,
        )

    up = remote(
        ext.at[HALF:2 * HALF], ext.at[HALF + band:], halo_ss.at[0], halo_rs.at[0],
        (dp, jnp.maximum(sp - 1, 0)),
    )
    down = remote(
        ext.at[band:HALF + band], ext.at[0:HALF], halo_ss.at[1], halo_rs.at[1],
        (dp, jnp.minimum(sp + 1, n_space - 1)),
    )

    @pl.when(sp > 0)
    def _():
        up.start()

    @pl.when(sp < n_space - 1)
    def _():
        down.start()

    def block(k_index, size):
        return pl.ds(pl.multiple_of(k_index * size, size), size)

    def far_first(count):
        return sorted(range(1, count), key=lambda k: -min(k, count - k))

    def exchange(src, dst, ss, rs, count, me, size, device):
        def begin():
            for k in far_first(count):
                there = block((me + k) % count, size)
                remote(src.at[there], dst.at[block(me, size)], ss, rs, device(k)).start()
            dst[block(me, size)] = src[block(me, size)]

        others = pl.ds(0, (count - 1) * size)
        return begin, remote(src.at[others], dst.at[others], ss, rs, (dp, partner))

    grads_y, came_y = exchange(sgy, rgy, gy_ss, gy_rs, NY, y, yrows, ydev)
    grads_z, came_z = exchange(sgz, rgz, gz_ss, gz_rs, nz, z, zrows, zdev)
    grads_y()

    for i in (3, 4, 5):
        loads[i].wait()
    at = lax.broadcasted_iota(jnp.int32, (width, 128), 0)

    def convolve(r, lanes, count, source):
        acc = [None] * KS
        for i in range(count):
            e = source(r, i)
            line = ext[e, :, lanes].astype(F32)
            taps = dwk[e - r, :, lanes]
            for dx in range(KS):
                term = line * taps[dx:dx + 1]
                acc[dx] = term if i == 0 else acc[dx] + term
        total = acc[HALF]
        for dx in range(KS):
            shift = dx - HALF
            if shift:
                moved = pltpu.roll(acc[dx], -shift % width, 0)
                inside = (at + shift >= 0) & (at + shift < width)
                total = total + jnp.where(inside, moved, 0.0)
        return total

    @pl.loop(0, chans // 128)
    def _(j):
        lanes = block(j, 128)

        @pl.loop(0, band)
        def _(r):
            own = convolve(r, lanes, band, lambda r, i: HALF + i)
            mixed[block(r, width), lanes] = own + bias[:, lanes]

    q_z, q_y, q_r = fields(ii, nz, NY, CAP)
    middle[...] = onehot(jj == q_y * yrows + q_z * CAP + q_r)
    loads[2].wait()
    named = jnp.broadcast_to(owner[...].astype(F32), (slots, slots))
    named_col = jnp.sum(jnp.where(ii == jj, named, 0.0), axis=1, keepdims=True)
    rank = jnp.sum(
        jnp.where((named_col == named) & (ii < jj), 1.0, 0.0), axis=0, keepdims=True
    )
    slot = jnp.broadcast_to((owner[...] * CAP).astype(F32) + rank, (slots, slots))
    perm[...] = onehot(ii.astype(F32) == slot)
    u_core, u_x, u_i = fields(ii, CORES, nx, tb)
    pos_col = jnp.sum(
        jnp.where(jj == (u_x * CORES + u_core) * tb + u_i, slot, 0.0), axis=1, keepdims=True
    )
    pick[...] = onehot(jj.astype(F32) == pos_col)

    @pl.when(sp < n_space - 1)
    def _():
        up.wait_recv()

    @pl.when(sp > 0)
    def _():
        down.wait_recv()

    @pl.loop(0, chans // 128)
    def _(j):
        lanes = block(j, 128)

        @pl.loop(0, band, unroll=True)
        def _(r):
            at_rows = block(r, width)
            mixed[at_rows, lanes] += convolve(
                r, lanes, HALF, lambda r, i: r + i + band * ((r + i) // HALF)
            )

    @pl.loop(0, band, unroll=True)
    def _(r):
        at_rows = block(r, width)
        normed, inv = norm(mixed[at_rows, :])
        normed1[at_rows, :] = normed
        inv1[at_rows, :] = inv
        first[at_rows, :] = (normed * mixg[...]).astype(BF16)

    loads[6].wait()

    @pl.loop(0, hid // 256, unroll=True)
    def _(j):
        cols = block(j, 256)
        pre = dot(first[...], wexp[:, cols])
        cumulative = 0.5 * (1.0 + lax.erf(pre * 0.7071067811865476))
        density = jnp.exp(-0.5 * pre * pre) * 0.3989422804014327
        hidden[:, cols] = (pre * cumulative).astype(BF16)
        slope[:, cols] = cumulative + pre * density

    loads[7].wait()

    @pl.loop(0, chans // 256, unroll=True)
    def _(j):
        cols = block(j, 256)
        proj[:, cols] = dot(hidden[...], wred[:, cols])

    loads[8].wait()
    loads[9].wait()

    @pl.loop(0, band, unroll=True)
    def _(r):
        at_rows = block(r, width)
        residual = ext[HALF + r].astype(F32)
        normed, inv = norm(residual + scale[...] * proj[at_rows, :])
        inv2[at_rows, :] = jnp.broadcast_to(inv, (width, 128))
        for c in range(chans // 128):
            lanes = slice(c * 128, (c + 1) * 128)
            normed2[c, at_rows, :] = normed[:, lanes]
            second[c, at_rows, :] = normed[:, lanes] * downg[:, lanes]

    def spots(a, b, big_r):
        return pl.ds((2 * big_r + a) * width + b, width // 2, stride=2)

    for a in range(2):
        for b in range(2):
            for c in range(chans // 128):
                lanes = slice((2 * a + b) * chans + c * 128, (2 * a + b) * chans + (c + 1) * 128)
                lines = [second[c, spots(a, b, big_r), :] for big_r in range(band // 2)]
                gathered[block(sp, tb), lanes] = jnp.concatenate(lines, axis=0).astype(BF16)

    right, left, over = (x + 1) % nx, (x + nx - 1) % nx, (x + 2) % nx

    def held(chip, h):
        return gathered.at[pl.ds(pl.multiple_of((chip * CORES + core) * tb + h * (tb // 2), tb // 2), tb // 2)]

    def ag(i, chip, h, target):
        return remote(
            held(chip, h), held(chip, h), ag_ss.at[i], ag_rs.at[i], (dp, target * CORES + core)
        )

    def fw(i, chip, h):
        return remote(held(chip, h), held(chip, h), fw_ss.at[i], fw_rs.at[i], (dp, partner))

    sends = [
        ag(0, x, 0, right), ag(1, x, 1, left), ag(2, x, 1, right), ag(3, x, 0, left),
        ag(4, left, 0, right), ag(5, right, 1, left),
    ]
    passed = [
        fw(0, left, 0), fw(1, right, 1), fw(2, left, 1), fw(3, right, 0),
        fw(4, over, 0), fw(5, over, 1), fw(6, x, 0), fw(7, x, 1),
    ]
    for i in range(4):
        sends[i].start()
    passed[6].start()
    passed[7].start()

    pl.semaphore_wait(known, len(near_z))
    came_y.wait_recv()
    sgz[...] = dot(middle[...], rgy[...]).astype(BF16)
    grads_z()

    for i in range(4):
        sends[i].wait_recv()
        if i < 2:
            sends[4 + i].start()
        passed[i].start()

    came_z.wait_recv()
    gtok[...] = dot(pick[...], rgz[...]).astype(BF16)
    loads[10].wait()
    half = nx * tb
    parts = [slice(q * chans, (q + 1) * chans) for q in range(4)]

    def pair(q):
        return remote(pair_s.at[q], pair_r.at[q], pair_ss.at[q], pair_rs.at[q], (dp, partner))

    hb = tb // 2

    def ring(q, i):
        first_row, target = (
            (0, right), (hb, left), (tb + hb, right), (tb, left), (2 * tb, right),
            (2 * tb + hb, left),
        )[i]
        at_rows = pl.ds(first_row, hb)
        return remote(
            rs_s.at[q, at_rows], rs_r.at[q, at_rows], rs_ss.at[q, i], rs_rs.at[q, i],
            (dp, target * CORES + core),
        )

    def term(q, chip, h):
        at_rows = pl.ds(pl.multiple_of(chip * tb + h * hb, hb), hb)
        return own_f[q, at_rows, :] + pair_r[q, at_rows, :].astype(F32)

    for q in range(4):
        pair_s[q] = dot(gtok[block(1 - core, half), :], wdt[:, parts[q]]).astype(BF16)
        pair(q).start()

    for i in range(4, 6):
        sends[i].wait_recv()
        passed[i].start()

    for q in range(4):
        own_f[q] = dot(gtok[block(core, half), :], wdt[:, parts[q]])
        pair(q).wait_recv()
        rs_s[q, 0:hb, :] = term(q, over, 0).astype(BF16)
        ring(q, 0).start()
        rs_s[q, hb:tb, :] = term(q, over, 1).astype(BF16)
        ring(q, 1).start()
        rs_s[q, tb + hb:2 * tb, :] = term(q, right, 1).astype(BF16)
        ring(q, 2).start()
        rs_s[q, tb:tb + hb, :] = term(q, left, 0).astype(BF16)
        ring(q, 3).start()

    for copy in passed:
        copy.wait_recv()
    tokens = dot_nt(gathered[:, 0:chans], wdt[:, 0:chans])
    for q in range(1, 4):
        cols = slice(q * chans, (q + 1) * chans)
        tokens = tokens + dot_nt(gathered[:, cols], wdt[:, cols])
    st[...] = dot(perm[...], tokens.astype(BF16)).astype(BF16).reshape(slots // CAP, CAP, group)

    def token(far_y, far_z):
        def away(far, count):
            return (count // 2 + (1 - 2 * (far % 2)) * ((far + 1) // 2) + count) % count

        o = (z + away(far_z, nz)) % nz * NY + (y + away(far_y, NY)) % NY
        remote(st.at[o], rt.at[dp], t_ss, t_rs, (o, sp)).start()

    @pl.loop(0, NY - 1)
    def _(far_y):
        @pl.loop(0, nz, unroll=nz)
        def _(far_z):
            token(far_y, far_z)

    @pl.loop(0, nz - 1, unroll=nz - 1)
    def _(far_z):
        token(NY - 1, far_z)

    rt[dp] = st[dp]

    for q in range(4):
        ring(q, 0).wait_recv()
        rs_s[q, 2 * tb:2 * tb + hb, :] = (
            term(q, right, 0) + rs_r[q, 0:hb, :].astype(F32)
        ).astype(BF16)
        ring(q, 4).start()
        ring(q, 1).wait_recv()
        rs_s[q, 2 * tb + hb:3 * tb, :] = (
            term(q, left, 1) + rs_r[q, hb:tb, :].astype(F32)
        ).astype(BF16)
        ring(q, 5).start()

    here = block(x, tb)
    gain = downg[...]
    for a in range(2):
        for b in range(2):
            q = 2 * a + b
            grad = own_f[q, here, :] + pair_r[q, here, :].astype(F32)
            for i in range(2, 6):
                ring(q, i).wait_recv()
            for slot_at in (tb, 2 * tb):
                grad = grad + rs_r[q, slot_at:slot_at + tb, :].astype(F32)
            normed = jnp.concatenate([
                jnp.concatenate(
                    [normed2[c, spots(a, b, big_r), :] for c in range(chans // 128)], axis=1
                ) for big_r in range(band // 2)
            ], axis=0)
            inv = jnp.concatenate(
                [inv2[spots(a, b, big_r), :] for big_r in range(band // 2)], axis=0
            )
            grad = norm_back(grad, normed, inv[:, 0:1], gain) * scale[...]
            for big_r in range(band // 2):
                for c in range(chans // 128):
                    second[c, spots(a, b, big_r), :] = grad[
                        big_r * (width // 2):(big_r + 1) * (width // 2), c * 128:(c + 1) * 128
                    ]
    for c in range(chans // 128):
        gscaled[:, c * 128:(c + 1) * 128] = second[c].astype(BF16)

    @pl.loop(0, hid // 256, unroll=True)
    def _(j):
        cols = block(j, 256)
        gpre[:, cols] = (dot_nt(gscaled[...], wred[cols, :]) * slope[:, cols]).astype(BF16)

    @pl.loop(0, chans // 256, unroll=True)
    def _(j):
        cols = block(j, 256)
        gfirst[:, cols] = dot_nt(gpre[...], wexp[cols, :])

    @pl.loop(0, band, unroll=True)
    def _(r):
        at_rows = block(r, width)
        grad = norm_back(gfirst[at_rows, :], normed1[at_rows, :], inv1[at_rows, :], mixg[...])
        grad_o[at_rows, :] = grad.astype(BF16)

    every = slots // CAP - 1
    came = remote(st.at[0:every], rt.at[0:every], t_ss, t_rs, (dp, partner))
    came.wait_recv()
    tok_o[...] = dot_tn(rt[...].reshape(slots, group), onehot(ii == jj)).astype(BF16)

    @pl.when(sp > 0)
    def _():
        up.wait_send()

    @pl.when(sp < n_space - 1)
    def _():
        down.wait_send()

    for q in range(4):
        pair(q).wait_send()
        for i in range(6):
            ring(q, i).wait_send()
    for copy in (*sends, *passed):
        copy.wait_send()
    came.wait_send()
    came_y.wait_send()
    came_z.wait_send()


def on_device(
    section_three, dw_kernel, dw_bias, mix_gain, w_expand, w_reduce, layer_scale, down_gain,
    w_down, owner_table, grad_packed,
):
    _, band, width, chans = section_three.shape
    hid = w_expand.shape[1]
    group = w_down.shape[1]
    slots = grad_packed.shape[1]
    n_dp, n_space = lax.axis_size("dp"), lax.axis_size("space")
    nz, nx = n_dp // NY, n_space // CORES
    rows = band * width
    tb = rows // 4
    dims = (nz, nx, band, width, chans, hid, group, slots)
    vmem = pltpu.VMEM
    dma = pltpu.SemaphoreType.DMA
    scratch = [
        vmem((band + 2 * HALF, width, chans), BF16),
        vmem((KS, KS, chans), F32), vmem((1, chans), F32), vmem((1, chans), F32),
        vmem((chans, hid), BF16), vmem((hid, chans), BF16), vmem((1, chans), F32),
        vmem((1, chans), F32), vmem((group, 4 * chans), BF16), vmem((1, slots), jnp.int32),
        vmem((group, slots), BF16),
        *[vmem((slots, slots), BF16)] * 3,
        *[vmem((slots, group), BF16)] * 4, *[vmem((slots // CAP, CAP, group), BF16)] * 2,
        vmem((rows, chans), F32), vmem((rows, chans), F32), vmem((rows, 1), F32),
        vmem((rows, chans), BF16), vmem((rows, hid), F32), vmem((rows, hid), BF16),
        vmem((rows, hid), BF16), vmem((rows, chans), F32),
        vmem((chans // 128, rows, 128), F32), vmem((rows, 128), F32),
        vmem((chans // 128, rows, 128), F32),
        vmem((n_space * tb, 4 * chans), BF16), vmem((slots, group), BF16),
        vmem((4, nx * tb, chans), BF16), vmem((4, nx * tb, chans), BF16),
        vmem((4, nx * tb, chans), F32),
        vmem((4, 3 * tb, chans), BF16), vmem((4, 3 * tb, chans), BF16),
        vmem((rows, chans), F32), vmem((rows, chans), BF16),
        dma((11,)), dma((2,)), dma((2,)),
        dma, dma, dma, dma, dma, dma, dma((6,)), dma((6,)), dma((8,)), dma((8,)), dma((4,)), dma((4,)),
        dma((4, 6)), dma((4, 6)), pltpu.SemaphoreType.REGULAR,
    ]
    anywhere = pl.BlockSpec(memory_space=pl.ANY)
    inside = pl.BlockSpec(memory_space=pltpu.VMEM)
    macs = rows * chans * hid * 4 + 2 * slots * group * 4 * chans
    tok, grad = pl.pallas_call(
        functools.partial(kernel, dims),
        out_shape=(vmem((group, slots), BF16), vmem((rows, chans), BF16)),
        in_specs=[anywhere] * 11,
        out_specs=(inside, inside),
        scratch_shapes=scratch,
        compiler_params=pltpu.CompilerParams(
            collective_id=0, has_side_effects=True, vmem_limit_bytes=56 * 2**20
        ),
        cost_estimate=pl.CostEstimate(
            flops=2 * macs, bytes_accessed=8 * 2**20, transcendentals=2 * rows * hid
        ),
    )(
        section_three[0], dw_kernel, dw_bias, mix_gain, w_expand, w_reduce,
        layer_scale, down_gain, w_down.T, owner_table[:, :, 0], grad_packed[0].T,
    )
    return tok.T[None], grad.reshape(1, band, width, chans)


def solution(mesh):
    in_specs = (
        P("dp", "space", None, None), P(), P(), P(), P(), P(), P(), P(), P(None, "space"),
        P("dp", None, None), P("dp", None, "space"),
    )
    out_specs = (P("dp", None, "space"), P("dp", "space", None, None))
    return jax.shard_map(
        on_device, mesh=mesh, in_specs=in_specs, out_specs=out_specs, check_vma=False
    )
```
